32 devices in a mesh: region: 4 (over x, core), blk: 8 (over z, y).
Axes of the slice: x: 2, y: 2, z: 4, core: 2. Of those that a mesh axis runs over, the one named last changes fastest.
Arguments:
- velocity: float32 [3, 64, 256, 256], P(None, 'region', 'blk'), may hold values from -5 to 5
- viscosity: float32 [64, 256, 256], P('region', 'blk'), may hold values from 0.02 to 0.1
- match_cell: int32 [32768], P(('region', 'blk')), may hold values from 0 to 131071
- wall_cell: int32 [32768], P(('region', 'blk')), may hold values from 0 to 131071
- match_dest: int32 [32768, 1], P(('region', 'blk')), may hold values from 0 to 31; in each aligned block of 1024 rows (0 to 1023, 1024 to 2047, ...) at most 64 rows name the same one
- match_count: int32 [32], P(('region', 'blk')), may hold values from 1 to 1024, 26214 in all
- wall_geom: float32 [4, 65536], P(None, ('region', 'blk')), may hold values from -1 to 1, as said below
Outputs:
- advanced: float32 [3, 64, 256, 256], P(None, 'region', 'blk')
- wall_log_stress: float32 [32768], P(('region', 'blk'))
The draws below stay inside these ranges and needn't reach their ends.
Inputs may be any that keep to these rules, and one draw needn't show every extreme that they name: `match_dest`: among the 1024 rows of one device at most 64 name the same owner, and some device reaches 64. The first match_count rows of a device's matching points are live; some device has all 1024 live. `match_cell`: local cell index of the device's 16 x 32 x 256 cells. `wall_cell`: local cell index of the device's 16 x 32 x 256 cells. `wall_geom`: row 0 lies in 0.02 to 0.3; rows 1 to 3 have magnitudes 0.3 to 1.
All inputs are finite; a program needn't handle non-finite values.
Results may differ from the reference program's by a relative error of at most 0.0003.
Values sent between devices are 32-bit elements; how exact they have to be, the bound alone decides.
A program may use at most 192 MiB of HBM per device.

```python
import math
import jax
import jax.numpy as jnp
import numpy as np
from jax import lax

CX = 16
CY = 32
CZ = 256
MP_DEV = 1024
NEWTON = 2
NX = 64
NY = 256
CELLS_DEV = 131072
MATCH = 32768
CAP = 64
FACES = 65536
LIVE = 26214
N_REGION = 4
N_BLK = 8
DEVICES = 32


def draw_wall_geom(key, part):
    key_dist, key_size, key_sign = jax.random.split(key, 3)
    distance = jnp.exp(jax.random.uniform(key_dist, (1, FACES), jnp.float32, math.log(0.02), math.log(0.3)))
    magnitude = jax.random.uniform(key_size, (3, FACES), jnp.float32, 0.3, 1.0)
    signs = (jax.random.randint(key_sign, (3, FACES), 0, 2) * 2 - 1).astype(jnp.float32)
    return jnp.concatenate([distance, magnitude * signs], axis=0)


def with_ends(array, key, least, top_value):
    longest = array.shape.index(max(array.shape))
    spots = []
    for shift in (0, 1):
        where = [jax.random.randint(jax.random.fold_in(key, axis), (), 0, length) for axis, length in enumerate(array.shape)]
        where[longest] = (where[longest] + shift) % array.shape[longest]
        spots.append(tuple(where))
    return array.at[spots[0]].set(least).at[spots[1]].set(top_value)


def shard_levels(key, shape, shards, least, top_value):
    gain = 1.0
    for position, parts in shards:
        steps = jax.random.uniform(jax.random.fold_in(jax.random.fold_in(key, 6), position), (parts,), jnp.float32, least / len(shards), top_value / len(shards))
        gain = gain * jnp.repeat(jnp.exp(steps), shape[position] // parts).reshape((-1,) + (1,) * (len(shape) - 1 - position))
    return gain


def split_up(number_of, total, limit, slope):
    portions = [(1 << 20) // math.isqrt(standing ** slope) + 1 for standing in range(2, number_of + 1)]
    surplus, given = total - limit - (number_of - 1), [1] * (number_of - 1)
    while surplus > 0:
        movable = [i for i in range(number_of - 1) if given[i] < limit]
        whole, budget = sum([portions[i] for i in movable]), surplus
        for i in movable:
            extra = min(limit - given[i], max(1, budget * portions[i] // whole), surplus)
            given[i] = given[i] + extra
            surplus = surplus - extra
    return np.array([limit] + given)


def ragged_sizes(stream_key, amount, total, bound, slope):
    if amount == 2:
        one = jax.random.randint(stream_key, (), max(1, total - bound), min(bound, total - 1) + 1)
        return jnp.stack([one, total - one])
    lengths = jnp.asarray(split_up(amount, total, bound, slope), jnp.int32)
    couples = (amount - 1) // 2
    source_of, taker = lengths[1:1 + 2 * couples:2], lengths[2:2 + 2 * couples:2]
    room = jnp.minimum(source_of - 1, bound - taker)
    passed = jax.random.randint(jax.random.fold_in(stream_key, 1), (couples,), 0, 1 << 20) % (room + 1)
    lengths = lengths.at[1:1 + 2 * couples:2].set(source_of - passed).at[2:2 + 2 * couples:2].set(taker + passed)
    return lengths[jax.random.permutation(jax.random.fold_in(stream_key, 2), amount)]


def deal_out(own_key, own, number, rows, count, top, bound, lean):
    order = jax.random.permutation(own_key, count)
    heavy_load, usual = load_shares(count, rows * top, bound, lean, True), load_shares(count, rows * top, bound, lean, False)
    places = jnp.arange(count)

    def named(tallies, turn):
        used = int((tallies > 0).sum())
        fixed = max(1, used // 4)
        passed = fixed + (places - fixed + turn * (used - fixed)) % max(1, count - fixed)
        return jnp.zeros((count,), jnp.int32).at[order[jnp.where(places < fixed, places, passed)]].set(jnp.asarray(tallies, jnp.int32))

    tallies = jnp.where(number % 4 == 0, named(heavy_load, number // 4), named(usual, number - number // 4 - 1))
    mixed = jax.random.permutation(jax.random.fold_in(own, 3), count)
    donor, taker = mixed[0:count // 2 * 2:2], mixed[1:count // 2 * 2:2]
    slack = jnp.minimum(tallies[donor] - 1, bound - tallies[taker]) // 2
    slack = jnp.where((donor == order[0]) | (taker == order[0]) | (tallies[taker] == 0), 0, jnp.maximum(slack, 0))
    passed = jax.random.randint(jax.random.fold_in(own, 4), (count // 2,), 0, 1 << 20) % (slack + 1)
    tallies = tallies.at[donor].add(-passed).at[taker].add(passed)
    labels = jnp.searchsorted(jnp.cumsum(tallies), jnp.arange(rows * top), side="right").astype(jnp.int32)
    grid = labels.reshape(top, rows).T
    grid = grid[jax.random.permutation(jax.random.fold_in(own, 1), rows)]
    turn = jax.random.randint(jax.random.fold_in(own, 2), (rows, 1), 0, top)
    return jnp.take_along_axis(grid, (jnp.arange(top)[None, :] + turn) % top, axis=1)


def load_shares(count, total, bound, slope, full):
    weights = [(1 << 20) // math.isqrt(grade ** slope) + 1 for grade in range(1, count + 1)]
    largest = bound if full else min(bound, max(-(-total // count), total * weights[0] // sum(weights)))
    least = 1 if total - largest >= count - 1 else 0
    given, surplus = [largest] + [least] * (count - 1), total - largest - least * (count - 1)
    while surplus > 0:
        candidates = [i for i in range(1, count) if given[i] < largest] or [i for i in range(1, count) if given[i] < bound]
        mass, remaining = sum([weights[i] for i in candidates]), surplus
        for i in candidates:
            addition = min(bound - given[i], max(1, remaining * weights[i] // mass), surplus)
            given[i] = given[i] + addition
            surplus = surplus - addition
    return np.array(given)


def bell_draw(key, dims, scale, bound, cuts=(), kind=jnp.bfloat16):
    values = scale * jax.random.normal(key, dims, jnp.float32)
    if cuts:
        values = values * shard_levels(key, dims, cuts, -0.22, 0.18)
    return jnp.clip(values, -bound, bound).astype(kind)


def setup_inputs(seed: int = 0) -> dict:
    keys = jax.random.split(jax.random.key(seed), 8)
    velocity = bell_draw(keys[0], (3, NX, NY, CZ), 1.0, 5.0, ((1, 4), (2, 8)), jnp.float32)
    viscosity = jnp.clip(jnp.exp(math.log(0.1) - 1.609438 * jax.random.uniform(keys[1], (NX, NY, CZ), jnp.float32) ** shard_levels(keys[1], (NX, NY, CZ), ((0, 4), (1, 8)), -0.2, 0.2)), 0.02, 0.1)
    match_cell = with_ends(jax.random.randint(keys[2], (MATCH,), 0, CELLS_DEV), jax.random.fold_in(keys[2], 1), 0, CELLS_DEV - 1).astype(jnp.int32)
    wall_cell = with_ends(jax.random.randint(keys[3], (MATCH,), 0, CELLS_DEV), jax.random.fold_in(keys[3], 1), 0, CELLS_DEV - 1).astype(jnp.int32)
    match_dest_keys = jax.random.split(jax.random.fold_in(keys[4], 1), MATCH // MP_DEV)
    match_dest_turns = jax.random.permutation(jax.random.fold_in(keys[4], 3), MATCH // MP_DEV)
    match_dest = jax.vmap(lambda own, number: deal_out(jax.random.fold_in(keys[4], 2), own, number, MP_DEV, DEVICES, 1, CAP, 2))(match_dest_keys, match_dest_turns).reshape((MATCH, 1))
    match_count = ragged_sizes(keys[5], DEVICES, LIVE, MP_DEV, 2).astype(jnp.int32)
    wall_geom = draw_wall_geom(jax.random.fold_in(keys[7], 71), 0)
    return dict(velocity=velocity, viscosity=viscosity, match_cell=match_cell, wall_cell=wall_cell, match_dest=match_dest, match_count=match_count, wall_geom=wall_geom)


KAPPA = 0.41
DAMPING = 26.0
NU_WALL = 0.0002
WALL_DY = 0.0005
TIME_STEP = 0.1
SPEED_FLOOR = 0.5
GUESS_RATIO = 14.0

def profile_table():
    fraction = jnp.arange(32, dtype=jnp.float32) / 31.0
    heights = fraction * fraction
    upper_end = jnp.concatenate([heights[1:], heights[-1:]])
    lower_end = jnp.concatenate([heights[:1], heights[:-1]])
    return (heights, 0.5 * (upper_end - lower_end))

def log_integral(log_speed, distance):
    heights, weights = profile_table()
    speed_now = jnp.exp(log_speed)[None, :]
    height = heights[:, None] * distance[None, :]
    van_driest = 1.0 - jnp.exp(-height * speed_now / (NU_WALL * DAMPING))
    eddy_visc = KAPPA * height * speed_now * van_driest * van_driest
    integrand = weights[:, None] * distance[None, :] * speed_now * speed_now / (NU_WALL + eddy_visc)
    return jnp.log(lax.optimization_barrier(jnp.sum(integrand, axis=0)))

def wall_solve(samples, geometry):
    distance = geometry[0]
    normal = geometry[1:4]
    normal = normal / jnp.sqrt(lax.optimization_barrier(jnp.sum(normal * normal, axis=0)))[None]
    normal_part = lax.optimization_barrier(jnp.sum(samples * normal, axis=0))
    tangent = samples - normal_part[None] * normal
    tangent_speed = jnp.maximum(jnp.sqrt(lax.optimization_barrier(jnp.sum(tangent * tangent, axis=0))), SPEED_FLOOR)
    target = jnp.log(tangent_speed)
    log_speed = target - jnp.log(GUESS_RATIO)
    slope_of = jax.grad(lambda values: jnp.sum(log_integral(values, distance)))
    for newton_step in range(NEWTON):
        log_speed = log_speed - (log_integral(log_speed, distance) - target) / slope_of(log_speed)
    stress = jnp.exp(2.0 * log_speed)
    return jnp.concatenate([(-stress / tangent_speed)[None] * tangent, (2.0 * log_speed)[None]], axis=0)

def tendency(padded, section_field, viscosity, forcing):
    extent = section_field.shape

    def window(axis_dim, offset):
        starts = [0, 2, 2, 2]
        starts[axis_dim] = starts[axis_dim] + offset
        limits = [starts[index] + extent[index] for index in range(4)]
        return lax.slice(padded, starts, limits)
    advect = jnp.zeros_like(section_field)
    spread = jnp.zeros_like(section_field)
    for axis_dim in (1, 2, 3):
        ahead_one = window(axis_dim, 1)
        behind_one = window(axis_dim, -1)
        ahead_two = window(axis_dim, 2)
        behind_two = window(axis_dim, -2)
        gradient = (8.0 * (ahead_one - behind_one) - (ahead_two - behind_two)) / 12.0
        advect = advect + section_field[axis_dim - 1][None] * gradient
        spread = spread + (16.0 * (ahead_one + behind_one) - (ahead_two + behind_two) - 30.0 * section_field) / 12.0
    return viscosity[None] * spread - advect + forcing

def reference(velocity, viscosity, match_cell, wall_cell, match_dest, match_count, wall_geom):
    devices = N_REGION * N_BLK
    slot_count = devices * CAP
    targets = match_dest[:, 0].reshape(devices, MP_DEV)
    is_live = jnp.arange(MP_DEV, dtype=jnp.int32)[None, :] < match_count[:, None]

    def ranks_of(pair):
        owner_row, live_row = pair
        owners = (owner_row[:, None] == jnp.arange(devices, dtype=jnp.int32)[None, :]) & live_row[:, None]
        running = jnp.cumsum(owners.astype(jnp.int32), axis=0) - 1
        return lax.optimization_barrier(jnp.sum(jnp.where(owners, running, 0), axis=1)).astype(jnp.int32)
    bucket_rank = lax.map(ranks_of, (targets, is_live))
    source = jnp.arange(devices, dtype=jnp.int32)[:, None]
    face_index = jnp.where(is_live, targets * slot_count + source * CAP + bucket_rank, 0).reshape(-1)
    geometry = jnp.take(wall_geom, face_index, axis=1)
    region_of = source // N_BLK
    block_of = source % N_BLK

    def global_index(local_cells):
        local_cells = local_cells.reshape(devices, MP_DEV)
        first_ix = local_cells // (CY * CZ)
        second_ix = local_cells // CZ % CY
        third_ix = local_cells % CZ
        return (((region_of * CX + first_ix) * NY + block_of * CY + second_ix) * CZ + third_ix).reshape(-1)
    match_global = global_index(match_cell)
    wall_global = global_index(wall_cell)
    live_flat = is_live.reshape(-1)

    def section_terms(section_field):
        flat_field = section_field.reshape(3, -1)
        samples = jnp.take(flat_field, match_global, axis=1)
        solved = wall_solve(samples, geometry)
        stress = jnp.where(live_flat[None], solved[:3], 0.0)
        forcing = jnp.zeros_like(flat_field).at[:, wall_global].add(stress / WALL_DY)
        log_stress = jnp.where(live_flat, solved[3], 0.0)
        padded = jnp.pad(section_field, ((0, 0), (2, 2), (2, 2), (2, 2)))
        return (tendency(padded, section_field, viscosity, forcing.reshape(section_field.shape)), log_stress)
    rate_first, first_stress = section_terms(velocity)
    first = velocity + TIME_STEP * rate_first
    rate_second, log_stress = section_terms(first)
    advanced = 0.5 * velocity + 0.5 * (first + TIME_STEP * rate_second)
    return (advanced, log_stress)
```

```python
import functools

import jax
import jax.numpy as jnp
from jax import lax
from jax.experimental import pallas as pl
from jax.experimental.pallas import tpu as pltpu
from jax.sharding import PartitionSpec as P

NEWTON = 2
KAPPA = 0.41
DAMPING = 26.0
NU_WALL = 0.0002
WALL_DY = 0.0005
TIME_STEP = 0.1
SPEED_FLOOR = 0.5
GUESS_RATIO = 14.0
LEVELS = 32

MESH = pl.DeviceIdType.MESH
BF16 = jnp.bfloat16
F32 = jnp.float32


def split2(x):
    hi = x.astype(BF16)
    return hi, (x - hi.astype(F32)).astype(BF16)


def split3(x):
    hi = x.astype(BF16)
    rest = x - hi.astype(F32)
    mid = rest.astype(BF16)
    return hi, mid, (rest - mid.astype(F32)).astype(BF16)


def one_hot(index_row, count):
    rows = lax.broadcasted_iota(jnp.int32, (count, index_row.shape[1]), 0)
    return jnp.where(rows == index_row, 1.0, 0.0)


def kernel(
    n_region, n_blk, cap,
    v_hbm, visc_ref, mcell_ref, wcell_ref, dest_ref, count_ref, geom_ref,
    adv_ref, log_ref,
    w1, w2, force, geo, ysend, yrecv1, yrecv2,
    oh_match, oh_wall, k_match, k_wall, vsplit, wsplit, wgeo,
    load_sem, gsend, grecv, own_sem, hsend, hrecv,
):
    comps, nx, ny, nz = v_hbm.shape
    rows_n = nx * ny
    points = mcell_ref.shape[1]
    devices = n_region * n_blk
    r = lax.axis_index("region")
    b = lax.axis_index("blk")
    me = r * n_blk + b

    barrier = pltpu.get_barrier_semaphore()

    @pl.loop(0, devices)
    def _(d):
        @pl.when(d != me)
        def _():
            pl.semaphore_signal(barrier, inc=1, device_id=(d // n_blk, d % n_blk), device_id_type=MESH)

    load = pltpu.make_async_copy(v_hbm, w1.at[:, 2 : 2 + nx, 8 : 8 + ny, :], load_sem)
    load.start()
    has = (r > 0, r < n_region - 1, b > 0, b < n_blk - 1)
    peers = ((r - 1, b), (r + 1, b), (r, b - 1), (r, b + 1))

    for w, yrecv in ((w1, yrecv1), (w2, yrecv2)):
        @pl.when(jnp.logical_not(has[0]))
        def _():
            w[:, 0:2, 8 : 8 + ny, :] = jnp.zeros((comps, 2, ny, nz), F32)

        @pl.when(jnp.logical_not(has[1]))
        def _():
            w[:, nx + 2 : nx + 4, 8 : 8 + ny, :] = jnp.zeros((comps, 2, ny, nz), F32)

        @pl.when(jnp.logical_not(has[2]))
        def _():
            yrecv[0] = jnp.zeros((comps, nx, 2, nz), F32)

        @pl.when(jnp.logical_not(has[3]))
        def _():
            yrecv[1] = jnp.zeros((comps, nx, 2, nz), F32)

    pl.semaphore_wait(barrier, devices - 1)

    def geo_copy(d):
        at = pl.multiple_of((d * cap) // 128 * 128, 128)
        return pltpu.make_async_remote_copy(
            src_ref=geom_ref.at[:, pl.ds(at, 128)],
            dst_ref=geo.at[me],
            send_sem=gsend.at[d],
            recv_sem=grecv.at[me],
            device_id=(d // n_blk, d % n_blk),
            device_id_type=MESH,
        )

    @pl.loop(0, devices)
    def _(d):
        @pl.when(d != me)
        def _():
            geo_copy(d).start()

    my_at = pl.multiple_of((me * cap) // 128 * 128, 128)
    own = pltpu.make_async_copy(geom_ref.at[:, pl.ds(my_at, 128)], geo.at[me], own_sem)
    own.start()

    def halo_copies(section, w, yrecv, xsource):
        out = []
        for side in range(4):
            if side == 0:
                src, dst = xsource(0), w.at[:, nx + 2 : nx + 4, 8 : 8 + ny, :]
            elif side == 1:
                src, dst = xsource(nx - 2), w.at[:, 0:2, 8 : 8 + ny, :]
            elif side == 2:
                src, dst = ysend.at[section, 0], yrecv.at[1]
            else:
                src, dst = ysend.at[section, 1], yrecv.at[0]
            out.append(
                pltpu.make_async_remote_copy(
                    src_ref=src, dst_ref=dst,
                    send_sem=hsend.at[section, side], recv_sem=hrecv.at[section, side],
                    device_id=peers[side], device_id_type=MESH,
                )
            )
        return out

    halo1 = halo_copies(0, w1, yrecv1, lambda i: v_hbm.at[:, i : i + 2])
    halo2 = halo_copies(1, w2, yrecv2, lambda i: w2.at[:, i + 2 : i + 4, 8 : 8 + ny, :])

    def start(copies, sides):
        for side in sides:
            pl.when(has[side])(copies[side].start)

    def finish(copies):
        for side in range(4):
            pl.when(has[side])(copies[side].wait_send)
            pl.when(has[side ^ 1])(copies[side].wait_recv)

    start(halo1, (0, 1))
    load.wait()

    def stage_y(section, w):
        @pl.loop(0, nx)
        def _(i):
            for c in range(comps):
                ysend[section, 0, c, i] = w[c, 2 + i, 8:10, :]
                ysend[section, 1, c, i] = w[c, 2 + i, 6 + ny : 8 + ny, :]

    stage_y(0, w1)
    start(halo1, (2, 3))

    mcell = mcell_ref[...]
    wcell = wcell_ref[...]
    live = lax.broadcasted_iota(jnp.int32, (1, points), 1) < count_ref[...]
    oh_match[...] = one_hot(mcell // nz, rows_n).astype(BF16)
    wall_rows = one_hot(wcell // nz, rows_n).astype(BF16)
    oh_wall[:, 0:points] = wall_rows
    oh_wall[:, points : 2 * points] = wall_rows
    k_match[...] = one_hot(mcell % nz, nz)
    k_wall[...] = one_hot(wcell % nz, nz).astype(BF16)

    own_mask = jnp.where(
        (lax.broadcasted_iota(jnp.int32, (devices, points), 0) == dest_ref[...]) & live, 1.0, 0.0
    )
    tri_row = lax.broadcasted_iota(jnp.int32, (128, 256), 0)
    tri_col = lax.broadcasted_iota(jnp.int32, (128, 256), 1)
    tri = jnp.where((tri_row < tri_col) | (tri_col >= 128), 1.0, 0.0).astype(BF16)
    before = jnp.zeros((devices, 128), F32)
    ranks = []
    for j in range(points // 128):
        part = own_mask[:, j * 128 : (j + 1) * 128]
        sums = jnp.dot(part.astype(BF16), tri, preferred_element_type=F32)
        ranks.append(jnp.sum(part * (sums[:, :128] + before), axis=0, keepdims=True))
        before = before + sums[:, 128:]
    rank = jnp.concatenate(ranks, axis=1).astype(jnp.int32)
    offset = me * cap - (me * cap) // 128 * 128
    rank_mask = one_hot(rank + offset, 128)
    own_bf = own_mask.astype(BF16)
    own3 = jnp.concatenate([own_bf, own_bf, own_bf], axis=0)

    def samples_of(w):
        got = []
        for c in range(comps):
            hi, lo = split2(w[c, 2 : 2 + nx, 8 : 8 + ny, :].reshape(rows_n, nz))
            acc = lax.dot_general(hi, oh_match[...], (((0,), (0,)), ((), ())), preferred_element_type=F32)
            acc = acc + lax.dot_general(lo, oh_match[...], (((0,), (0,)), ((), ())), preferred_element_type=F32)
            got.append(jnp.sum(acc * k_match[...], axis=0, keepdims=True))
        return got

    samples = samples_of(w1)

    own.wait()

    @pl.loop(0, devices)
    def _(d):
        @pl.when(d != me)
        def _():
            copy = pltpu.make_async_remote_copy(
                src_ref=geom_ref.at[:, pl.ds(my_at, 128)],
                dst_ref=geo.at[d],
                send_sem=gsend.at[d],
                recv_sem=grecv.at[d],
                device_id=(d // n_blk, d % n_blk),
                device_id_type=MESH,
            )
            copy.wait_send()
            copy.wait_recv()

    records = []
    for c in range(4):
        hi, mid, lo = split3(geo[:, c, :])
        three = jnp.concatenate([hi, mid, lo], axis=0)
        chosen = lax.dot_general(three, own3, (((0,), (0,)), ((), ())), preferred_element_type=F32)
        records.append(jnp.sum(chosen * rank_mask, axis=0, keepdims=True))
    distance = records[0]
    inv = 1.0 / jnp.sqrt(records[1] * records[1] + records[2] * records[2] + records[3] * records[3])
    normal = [records[1] * inv, records[2] * inv, records[3] * inv]

    level = lax.broadcasted_iota(jnp.int32, (LEVELS, 1), 0).astype(F32)
    last = LEVELS - 1.0
    eta = (level / last) * (level / last)
    above = jnp.minimum(level + 1.0, last) / last
    below = jnp.maximum(level - 1.0, 0.0) / last
    weight = 0.5 * (above * above - below * below)
    log_distance = jnp.log(distance)

    def wall_solve(got):
        along = got[0] * normal[0] + got[1] * normal[1] + got[2] * normal[2]
        tangent = [got[c] - along * normal[c] for c in range(comps)]
        speed = jnp.sqrt(tangent[0] * tangent[0] + tangent[1] * tangent[1] + tangent[2] * tangent[2])
        speed = jnp.maximum(speed, SPEED_FLOOR)
        target = jnp.log(speed)
        s = target - jnp.log(GUESS_RATIO)
        for _ in range(NEWTON):
            z = eta * (distance * jnp.exp(s))
            a = z * (1.0 / (NU_WALL * DAMPING))
            e = jnp.exp(-a)
            damp = 1.0 - e
            kzd = (KAPPA * z) * damp
            eddy = kzd * damp
            inv_den = 1.0 / (NU_WALL + eddy)
            f = weight * inv_den
            slope = (eddy + 2.0 * kzd * (e * a)) * inv_den
            total = jnp.sum(f, axis=0, keepdims=True)
            bend = jnp.sum(f * slope, axis=0, keepdims=True)
            value = log_distance + 2.0 * s + jnp.log(total) - target
            s = s - value / (2.0 - bend / total)
        factor = -jnp.exp(2.0 * s) / speed / WALL_DY
        return [jnp.where(live, factor * t, 0.0) for t in tangent], jnp.where(live, 2.0 * s, 0.0)

    def scatter(stress):
        for c in range(comps):
            hi, lo = split2(stress[c])
            wsplit[:, 0:points] = k_wall[...] * hi
            wsplit[:, points : 2 * points] = k_wall[...] * lo
            out = lax.dot_general(
                oh_wall[...], wsplit[...], (((1,), (1,)), ((), ())), preferred_element_type=F32
            )
            force[c] = out.reshape(nx, ny, nz)

    stress, _ = wall_solve(samples)
    scatter(stress)
    finish(halo1)

    lane = lax.broadcasted_iota(jnp.int32, (ny, nz), 1)

    def put_y(w, yrecv):
        @pl.loop(0, nx)
        def _(i):
            for c in range(comps):
                w[c, 2 + i, 6:8, :] = yrecv[0, c, i]
                w[c, 2 + i, 8 + ny : 10 + ny, :] = yrecv[1, c, i]

    def rate(w, i):
        nu = visc_ref[i]
        n16 = nu * (16.0 / 12.0)
        n1 = nu * (1.0 / 12.0)
        center = [w[c, 2 + i, 8 : 8 + ny, :] for c in range(comps)]
        acc = [force[c, i] - (7.5 * nu) * center[c] for c in range(comps)]
        for axis in range(3):
            g8 = center[axis] * (8.0 / 12.0)
            g1 = center[axis] * (1.0 / 12.0)
            p1, m1, p2, m2 = n16 - g8, n16 + g8, g1 - n1, -(g1 + n1)
            if axis == 2:
                p1 = jnp.where(lane < nz - 1, p1, 0.0)
                m1 = jnp.where(lane >= 1, m1, 0.0)
                p2 = jnp.where(lane < nz - 2, p2, 0.0)
                m2 = jnp.where(lane >= 2, m2, 0.0)
            for c in range(comps):
                if axis == 0:
                    near = [w[c, 2 + i + s, 8 : 8 + ny, :] for s in (1, -1, 2, -2)]
                elif axis == 1:
                    near = [w[c, 2 + i, 8 + s : 8 + s + ny, :] for s in (1, -1, 2, -2)]
                else:
                    near = [pltpu.roll(center[c], s % nz, 1) for s in (-1, 1, -2, 2)]
                acc[c] = acc[c] + ((p1 * near[0] + m1 * near[1]) + (p2 * near[2] + m2 * near[3]))
        return center, acc

    put_y(w1, yrecv1)

    @pl.loop(0, nx)
    def _(i):
        center, acc = rate(w1, i)
        for c in range(comps):
            w2[c, 2 + i, 8 : 8 + ny, :] = center[c] + TIME_STEP * acc[c]

    start(halo2, (0, 1))
    stage_y(1, w2)
    start(halo2, (2, 3))
    stress, logs = wall_solve(samples_of(w2))
    log_ref[...] = logs
    scatter(stress)
    finish(halo2)
    put_y(w2, yrecv2)

    @pl.loop(0, nx)
    def _(i):
        center, acc = rate(w2, i)
        for c in range(comps):
            v = w1[c, 2 + i, 8 : 8 + ny, :]
            adv_ref[c, i] = 0.5 * v + 0.5 * (center[c] + TIME_STEP * acc[c])


def local(n_region, n_blk, velocity, viscosity, match_cell, wall_cell, match_dest, match_count, wall_geom):
    comps, nx, ny, nz = velocity.shape
    points = match_cell.shape[0]
    devices = n_region * n_blk
    cap = wall_geom.shape[1] // devices
    vmem = pl.BlockSpec(memory_space=pltpu.VMEM)
    field = pltpu.VMEM((comps, nx + 4, ny + 16, nz), F32)
    advanced, log_stress = pl.pallas_call(
        functools.partial(kernel, n_region, n_blk, cap),
        out_shape=(
            jax.ShapeDtypeStruct((comps, nx, ny, nz), F32),
            jax.ShapeDtypeStruct((1, points), F32),
        ),
        in_specs=[pl.BlockSpec(memory_space=pl.ANY)] + [vmem] * 6,
        out_specs=(vmem, vmem),
        scratch_shapes=[
            field,
            field,
            pltpu.VMEM((comps, nx, ny, nz), F32),
            pltpu.VMEM((devices, 4, 128), F32),
            pltpu.VMEM((2, 2, comps, nx, 2, nz), F32),
            pltpu.VMEM((2, comps, nx, 2, nz), F32),
            pltpu.VMEM((2, comps, nx, 2, nz), F32),
            pltpu.VMEM((nx * ny, points), BF16),
            pltpu.VMEM((nx * ny, 2 * points), BF16),
            pltpu.VMEM((nz, points), F32),
            pltpu.VMEM((nz, points), BF16),
            pltpu.VMEM((16, 128), BF16),
            pltpu.VMEM((nz, 2 * points), BF16),
            pltpu.VMEM((8, 128), F32),
            pltpu.SemaphoreType.DMA,
            pltpu.SemaphoreType.DMA((devices,)),
            pltpu.SemaphoreType.DMA((devices,)),
            pltpu.SemaphoreType.DMA,
            pltpu.SemaphoreType.DMA((2, 4)),
            pltpu.SemaphoreType.DMA((2, 4)),
        ],
        compiler_params=pltpu.CompilerParams(
            collective_id=0, has_side_effects=True, vmem_limit_bytes=56 * 1024 * 1024
        ),
    )(
        velocity,
        viscosity,
        match_cell.reshape(1, points),
        wall_cell.reshape(1, points),
        match_dest.reshape(1, points),
        match_count.reshape(1, 1),
        wall_geom,
    )
    return advanced, log_stress.reshape(points)


def solution(mesh):
    placed = (
        P(None, "region", "blk", None),
        P("region", "blk", None),
        P(("region", "blk")),
        P(("region", "blk")),
        P(("region", "blk"), None),
        P(("region", "blk")),
        P(None, ("region", "blk")),
    )
    return jax.shard_map(
        functools.partial(local, mesh.shape["region"], mesh.shape["blk"]),
        mesh=mesh,
        in_specs=placed,
        out_specs=(P(None, "region", "blk", None), P(("region", "blk"))),
        check_vma=False,
    )
```

```python
import functools

import jax
import jax.numpy as jnp
from jax import lax
from jax.experimental import pallas as pl
from jax.experimental.pallas import tpu as pltpu
from jax.sharding import PartitionSpec as P

NEWTON = 2
KAPPA = 0.41
DAMPING = 26.0
NU_WALL = 0.0002
WALL_DY = 0.0005
TIME_STEP = 0.1
SPEED_FLOOR = 0.5
GUESS_RATIO = 14.0
LEVELS = 32

MESH = pl.DeviceIdType.MESH
BF16 = jnp.bfloat16
F32 = jnp.float32


def split2(x):
    hi = x.astype(BF16)
    return hi, (x - hi.astype(F32)).astype(BF16)


def split3(x):
    hi = x.astype(BF16)
    rest = x - hi.astype(F32)
    mid = rest.astype(BF16)
    return hi, mid, (rest - mid.astype(F32)).astype(BF16)


def one_hot(index_row, count):
    rows = lax.broadcasted_iota(jnp.int32, (count, index_row.shape[1]), 0)
    return jnp.where(rows == index_row, 1.0, 0.0)


def kernel(
    n_region, n_blk, cap,
    v_hbm, visc_hbm, mcell_ref, wcell_ref, dest_ref, count_ref, geom_ref,
    adv_hbm, log_ref,
    visc_ref, adv_buf, w1, w2, force, geo, ysend, yrecv1, yrecv2,
    oh_match, oh_wall, k_match, k_wall, wsplit,
    load_sem, visc_sem, out_sem, gsend, grecv, own_sem, hsend, hrecv,
):
    comps, nx, ny, nz = v_hbm.shape
    rows_n = nx * ny
    points = mcell_ref.shape[1]
    devices = n_region * n_blk
    r = lax.axis_index("region")
    b = lax.axis_index("blk")
    me = r * n_blk + b

    barrier = pltpu.get_barrier_semaphore()

    @pl.loop(0, devices)
    def _(d):
        @pl.when(d != me)
        def _():
            pl.semaphore_signal(barrier, inc=1, device_id=(d // n_blk, d % n_blk), device_id_type=MESH)

    load = pltpu.make_async_copy(v_hbm, w1.at[:, 2 : 2 + nx, 8 : 8 + ny, :], load_sem)
    load.start()
    load_visc = pltpu.make_async_copy(visc_hbm, visc_ref, visc_sem)
    load_visc.start()
    has = (r > 0, r < n_region - 1, b > 0, b < n_blk - 1)
    peers = ((r - 1, b), (r + 1, b), (r, b - 1), (r, b + 1))

    for w, yrecv in ((w1, yrecv1), (w2, yrecv2)):
        @pl.when(jnp.logical_not(has[0]))
        def _():
            w[:, 0:2, 8 : 8 + ny, :] = jnp.zeros((comps, 2, ny, nz), F32)

        @pl.when(jnp.logical_not(has[1]))
        def _():
            w[:, nx + 2 : nx + 4, 8 : 8 + ny, :] = jnp.zeros((comps, 2, ny, nz), F32)

        @pl.when(jnp.logical_not(has[2]))
        def _():
            yrecv[0] = jnp.zeros((comps, nx, 2, nz), F32)

        @pl.when(jnp.logical_not(has[3]))
        def _():
            yrecv[1] = jnp.zeros((comps, nx, 2, nz), F32)

    mcell = mcell_ref[...]
    wcell = wcell_ref[...]
    live = lax.broadcasted_iota(jnp.int32, (1, points), 1) < count_ref[...]
    oh_match[...] = one_hot(mcell // nz, rows_n).astype(BF16)
    wall_rows = one_hot(wcell // nz, rows_n).astype(BF16)
    oh_wall[:, 0:points] = wall_rows
    oh_wall[:, points : 2 * points] = wall_rows
    k_match[...] = one_hot(mcell % nz, nz)
    k_wall[...] = one_hot(wcell % nz, nz).astype(BF16)

    own_mask = jnp.where(
        (lax.broadcasted_iota(jnp.int32, (devices, points), 0) == dest_ref[...]) & live, 1.0, 0.0
    )
    tri_row = lax.broadcasted_iota(jnp.int32, (128, 256), 0)
    tri_col = lax.broadcasted_iota(jnp.int32, (128, 256), 1)
    tri = jnp.where((tri_row < tri_col) | (tri_col >= 128), 1.0, 0.0).astype(BF16)
    before = jnp.zeros((devices, 128), F32)
    ranks = []
    for j in range(points // 128):
        part = own_mask[:, j * 128 : (j + 1) * 128]
        sums = jnp.dot(part.astype(BF16), tri, preferred_element_type=F32)
        ranks.append(jnp.sum(part * (sums[:, :128] + before), axis=0, keepdims=True))
        before = before + sums[:, 128:]
    rank = jnp.concatenate(ranks, axis=1).astype(jnp.int32)
    offset = me * cap - (me * cap) // 128 * 128
    rank_mask = one_hot(rank + offset, 128)
    own_bf = own_mask.astype(BF16)
    own3 = jnp.concatenate([own_bf, own_bf, own_bf], axis=0)

    pl.semaphore_wait(barrier, devices - 1)

    def geo_copy(d):
        at = pl.multiple_of((d * cap) // 128 * 128, 128)
        return pltpu.make_async_remote_copy(
            src_ref=geom_ref.at[:, pl.ds(at, 128)],
            dst_ref=geo.at[me],
            send_sem=gsend.at[d],
            recv_sem=grecv.at[me],
            device_id=(d // n_blk, d % n_blk),
            device_id_type=MESH,
        )

    @pl.loop(0, devices)
    def _(d):
        @pl.when(d != me)
        def _():
            geo_copy(d).start()

    my_at = pl.multiple_of((me * cap) // 128 * 128, 128)
    own = pltpu.make_async_copy(geom_ref.at[:, pl.ds(my_at, 128)], geo.at[me], own_sem)
    own.start()

    def halo_copies(section, w, yrecv, xsource):
        out = []
        for side in range(4):
            if side == 0:
                src, dst = xsource(0), w.at[:, nx + 2 : nx + 4, 8 : 8 + ny, :]
            elif side == 1:
                src, dst = xsource(nx - 2), w.at[:, 0:2, 8 : 8 + ny, :]
            elif side == 2:
                src, dst = ysend.at[section, 0], yrecv.at[1]
            else:
                src, dst = ysend.at[section, 1], yrecv.at[0]
            out.append(
                pltpu.make_async_remote_copy(
                    src_ref=src, dst_ref=dst,
                    send_sem=hsend.at[section, side], recv_sem=hrecv.at[section, side],
                    device_id=peers[side], device_id_type=MESH,
                )
            )
        return out

    halo1 = halo_copies(0, w1, yrecv1, lambda i: v_hbm.at[:, i : i + 2])
    halo2 = halo_copies(1, w2, yrecv2, lambda i: w2.at[:, i + 2 : i + 4, 8 : 8 + ny, :])

    def start(copies, sides):
        for side in sides:
            pl.when(has[side])(copies[side].start)

    def finish(copies):
        for side in range(4):
            pl.when(has[side])(copies[side].wait_send)
            pl.when(has[side ^ 1])(copies[side].wait_recv)

    start(halo1, (0, 1))
    load.wait()

    def stage_y(section, w):
        @pl.loop(0, nx, unroll=8)
        def _(i):
            for c in range(comps):
                ysend[section, 0, c, i] = w[c, 2 + i, 8:10, :]
                ysend[section, 1, c, i] = w[c, 2 + i, 6 + ny : 8 + ny, :]

    stage_y(0, w1)
    start(halo1, (2, 3))

    def samples_of(w):
        got = []
        for c in range(comps):
            hi, lo = split2(w[c, 2 : 2 + nx, 8 : 8 + ny, :].reshape(rows_n, nz))
            acc = lax.dot_general(hi, oh_match[...], (((0,), (0,)), ((), ())), preferred_element_type=F32)
            acc = acc + lax.dot_general(lo, oh_match[...], (((0,), (0,)), ((), ())), preferred_element_type=F32)
            got.append(jnp.sum(acc * k_match[...], axis=0, keepdims=True))
        return got

    samples = samples_of(w1)

    own.wait()

    @pl.loop(0, devices)
    def _(d):
        @pl.when(d != me)
        def _():
            copy = pltpu.make_async_remote_copy(
                src_ref=geom_ref.at[:, pl.ds(my_at, 128)],
                dst_ref=geo.at[d],
                send_sem=gsend.at[d],
                recv_sem=grecv.at[d],
                device_id=(d // n_blk, d % n_blk),
                device_id_type=MESH,
            )
            copy.wait_send()
            copy.wait_recv()

    records = []
    for c in range(4):
        hi, mid, lo = split3(geo[:, c, :])
        three = jnp.concatenate([hi, mid, lo], axis=0)
        chosen = lax.dot_general(three, own3, (((0,), (0,)), ((), ())), preferred_element_type=F32)
        records.append(jnp.sum(chosen * rank_mask, axis=0, keepdims=True))
    distance = records[0]
    inv = 1.0 / jnp.sqrt(records[1] * records[1] + records[2] * records[2] + records[3] * records[3])
    normal = [records[1] * inv, records[2] * inv, records[3] * inv]

    level = lax.broadcasted_iota(jnp.int32, (LEVELS, 1), 0).astype(F32)
    last = LEVELS - 1.0
    eta = (level / last) * (level / last)
    above = jnp.minimum(level + 1.0, last) / last
    below = jnp.maximum(level - 1.0, 0.0) / last
    weight = 0.5 * (above * above - below * below)
    log_distance = jnp.log(distance)

    def wall_solve(got):
        along = got[0] * normal[0] + got[1] * normal[1] + got[2] * normal[2]
        tangent = [got[c] - along * normal[c] for c in range(comps)]
        speed = jnp.sqrt(tangent[0] * tangent[0] + tangent[1] * tangent[1] + tangent[2] * tangent[2])
        speed = jnp.maximum(speed, SPEED_FLOOR)
        target = jnp.log(speed)
        s = target - jnp.log(GUESS_RATIO)
        for _ in range(NEWTON):
            z = eta * (distance * jnp.exp(s))
            a = z * (1.0 / (NU_WALL * DAMPING))
            e = jnp.exp(-a)
            damp = 1.0 - e
            kzd = (KAPPA * z) * damp
            eddy = kzd * damp
            inv_den = 1.0 / (NU_WALL + eddy)
            f = weight * inv_den
            slope = (eddy + 2.0 * kzd * (e * a)) * inv_den
            total = jnp.sum(f, axis=0, keepdims=True)
            bend = jnp.sum(f * slope, axis=0, keepdims=True)
            value = log_distance + 2.0 * s + jnp.log(total) - target
            s = s - value / (2.0 - bend / total)
        factor = -jnp.exp(2.0 * s) / speed / WALL_DY
        return [jnp.where(live, factor * t, 0.0) for t in tangent], jnp.where(live, 2.0 * s, 0.0)

    def scatter(stress):
        for c in range(comps):
            hi, lo = split2(stress[c])
            wsplit[:, 0:points] = k_wall[...] * hi
            wsplit[:, points : 2 * points] = k_wall[...] * lo
            out = lax.dot_general(
                oh_wall[...], wsplit[...], (((1,), (1,)), ((), ())), preferred_element_type=F32
            )
            force[c] = out.reshape(nx, ny, nz)

    stress, _ = wall_solve(samples)
    scatter(stress)
    finish(halo1)
    load_visc.wait()

    lane = lax.broadcasted_iota(jnp.int32, (ny, nz), 1)

    def put_y(w, yrecv):
        @pl.loop(0, nx, unroll=8)
        def _(i):
            for c in range(comps):
                w[c, 2 + i, 6:8, :] = yrecv[0, c, i]
                w[c, 2 + i, 8 + ny : 10 + ny, :] = yrecv[1, c, i]

    def rate(w, i):
        nu = visc_ref[i]
        n16 = nu * (16.0 / 12.0)
        n1 = nu * (1.0 / 12.0)
        center = [w[c, 2 + i, 8 : 8 + ny, :] for c in range(comps)]
        acc = [force[c, i] - (7.5 * nu) * center[c] for c in range(comps)]
        for axis in range(3):
            g8 = center[axis] * (8.0 / 12.0)
            g1 = center[axis] * (1.0 / 12.0)
            p1, m1, p2, m2 = n16 - g8, n16 + g8, g1 - n1, -(g1 + n1)
            if axis == 2:
                p1 = jnp.where(lane < nz - 1, p1, 0.0)
                m1 = jnp.where(lane >= 1, m1, 0.0)
                p2 = jnp.where(lane < nz - 2, p2, 0.0)
                m2 = jnp.where(lane >= 2, m2, 0.0)
            for c in range(comps):
                if axis == 0:
                    near = [w[c, 2 + i + s, 8 : 8 + ny, :] for s in (1, -1, 2, -2)]
                elif axis == 1:
                    near = [w[c, 2 + i, 8 + s : 8 + s + ny, :] for s in (1, -1, 2, -2)]
                else:
                    near = [pltpu.roll(center[c], s % nz, 1) for s in (-1, 1, -2, 2)]
                acc[c] = acc[c] + ((p1 * near[0] + m1 * near[1]) + (p2 * near[2] + m2 * near[3]))
        return center, acc

    put_y(w1, yrecv1)

    @pl.loop(0, nx)
    def _(i):
        center, acc = rate(w1, i)
        for c in range(comps):
            w2[c, 2 + i, 8 : 8 + ny, :] = center[c] + TIME_STEP * acc[c]

    start(halo2, (0, 1))
    stage_y(1, w2)
    start(halo2, (2, 3))
    stress, logs = wall_solve(samples_of(w2))
    for j in range(points // 128):
        log_ref[j : j + 1, :] = logs[:, j * 128 : (j + 1) * 128]
    scatter(stress)
    finish(halo2)
    put_y(w2, yrecv2)

    @pl.loop(0, nx)
    def _(i):
        center, acc = rate(w2, i)
        for c in range(comps):
            v = w1[c, 2 + i, 8 : 8 + ny, :]
            adv_buf[c, i] = 0.5 * v + 0.5 * (center[c] + TIME_STEP * acc[c])
        pltpu.make_async_copy(adv_buf.at[:, i], adv_hbm.at[:, i], out_sem).start()

    pltpu.make_async_copy(adv_buf, adv_hbm, out_sem).wait()


def hand_over(adv_in, log_in, adv_out, log_out, held, held_log, in_sems, out_sems):
    comps, nx = adv_in.shape[:2]
    step = nx // 4
    last = 4 * comps
    loads = [pltpu.make_async_copy(log_in, held_log, in_sems.at[last])]
    stores = [pltpu.make_async_copy(held_log, log_out, out_sems.at[last])]
    for c in range(comps):
        for j in range(4):
            part = (c, pl.ds(j * step, step))
            loads.append(pltpu.make_async_copy(adv_in.at[part], held.at[part], in_sems.at[4 * c + j]))
            stores.append(pltpu.make_async_copy(held.at[part], adv_out.at[part], out_sems.at[4 * c + j]))
    for load in loads:
        load.start()
    for load, store in zip(loads, stores):
        load.wait()
        store.start()
    for store in stores:
        store.wait()


def local(n_region, n_blk, velocity, viscosity, match_cell, wall_cell, match_dest, match_count, wall_geom):
    comps, nx, ny, nz = velocity.shape
    points = match_cell.shape[0]
    devices = n_region * n_blk
    cap = wall_geom.shape[1] // devices
    vmem = pl.BlockSpec(memory_space=pltpu.VMEM)
    hbm = pl.BlockSpec(memory_space=pl.ANY)
    field = pltpu.VMEM((comps, nx + 4, ny + 16, nz), F32)
    advanced, log_stress = pl.pallas_call(
        functools.partial(kernel, n_region, n_blk, cap),
        out_shape=(
            jax.ShapeDtypeStruct((comps, nx, ny, nz), F32),
            jax.ShapeDtypeStruct((points // 128, 128), F32),
        ),
        in_specs=[hbm, hbm] + [vmem] * 5,
        out_specs=(hbm, vmem),
        scratch_shapes=[
            pltpu.VMEM((nx, ny, nz), F32),
            pltpu.VMEM((comps, nx, ny, nz), F32),
            field,
            field,
            pltpu.VMEM((comps, nx, ny, nz), F32),
            pltpu.VMEM((devices, 4, 128), F32),
            pltpu.VMEM((2, 2, comps, nx, 2, nz), F32),
            pltpu.VMEM((2, comps, nx, 2, nz), F32),
            pltpu.VMEM((2, comps, nx, 2, nz), F32),
            pltpu.VMEM((nx * ny, points), BF16),
            pltpu.VMEM((nx * ny, 2 * points), BF16),
            pltpu.VMEM((nz, points), F32),
            pltpu.VMEM((nz, points), BF16),
            pltpu.VMEM((nz, 2 * points), BF16),
            pltpu.SemaphoreType.DMA,
            pltpu.SemaphoreType.DMA,
            pltpu.SemaphoreType.DMA,
            pltpu.SemaphoreType.DMA((devices,)),
            pltpu.SemaphoreType.DMA((devices,)),
            pltpu.SemaphoreType.DMA,
            pltpu.SemaphoreType.DMA((2, 4)),
            pltpu.SemaphoreType.DMA((2, 4)),
        ],
        compiler_params=pltpu.CompilerParams(
            collective_id=0, has_side_effects=True, vmem_limit_bytes=56 * 1024 * 1024
        ),
    )(
        velocity,
        viscosity,
        match_cell.reshape(1, points),
        wall_cell.reshape(1, points),
        match_dest.reshape(1, points),
        match_count.reshape(1, 1),
        wall_geom,
    )
    advanced, log_stress = pl.pallas_call(
        hand_over,
        out_shape=(
            jax.ShapeDtypeStruct(advanced.shape, F32),
            jax.ShapeDtypeStruct(log_stress.shape, F32),
        ),
        in_specs=[hbm, hbm],
        out_specs=(hbm, hbm),
        scratch_shapes=[
            pltpu.VMEM(advanced.shape, F32),
            pltpu.VMEM(log_stress.shape, F32),
            pltpu.SemaphoreType.DMA((4 * comps + 1,)),
            pltpu.SemaphoreType.DMA((4 * comps + 1,)),
        ],
    )(advanced, log_stress)
    return advanced, log_stress.reshape(points)


def solution(mesh):
    placed = (
        P(None, "region", "blk", None),
        P("region", "blk", None),
        P(("region", "blk")),
        P(("region", "blk")),
        P(("region", "blk"), None),
        P(("region", "blk")),
        P(None, ("region", "blk")),
    )
    return jax.shard_map(
        functools.partial(local, mesh.shape["region"], mesh.shape["blk"]),
        mesh=mesh,
        in_specs=placed,
        out_specs=(P(None, "region", "blk", None), P(("region", "blk"))),
        check_vma=False,
    )
```
